128 devices in a mesh: row: 16 (over x, y), col: 8 (over z, core).
Axes of the slice: x: 4, y: 4, z: 4, core: 2. Of those that a mesh axis runs over, the one named last changes fastest.
Arguments:
- momentum: bfloat16 [14336, 26624], P('row', 'col'), may hold values from -60 to 60
- gradient: bfloat16 [14336, 26624], P('row', 'col'), may hold values from -6 to 6
- right_factor: bfloat16 [26624, 256], P('col'), may hold values from -0.0390625 to 0.0390625
Outputs:
- new_momentum: bfloat16 [14336, 26624], P('row', 'col')
- new_factor: bfloat16 [26624, 256], P('col')
- update: bfloat16 [14336, 26624], P('row', 'col')
The draws below stay inside these ranges and needn't reach their ends.
All inputs are finite; a program needn't handle non-finite values.
Results may differ from the reference program's by a relative error of at most 0.012.
Values may be sent and summed in bfloat16 or wider, within the bound.
A program may use at most 128 MiB of HBM per device.

```python
import math
import jax
import jax.numpy as jnp
from jax import lax

M_ROWS = 14336
N_COLS = 26624
RANK = 256


def draw_momentum(key, part):
    key = jax.random.fold_in(key, 11)
    key_base, key_cols, key_rows = jax.random.split(key, 3)
    position = jnp.arange(N_COLS, dtype=jnp.float32) / N_COLS
    col_scale = jnp.exp(jnp.log(3.0) * (position - 0.5) + jax.random.uniform(key_cols, (N_COLS,), jnp.float32, -1.15, 1.15))
    row_scale = jnp.exp(jax.random.uniform(key_rows, (M_ROWS, 1), jnp.float32, -0.7, 0.7))
    base = jax.random.truncated_normal(key_base, -4.0, 4.0, (M_ROWS, N_COLS), jnp.float32)
    return (0.5 * base * row_scale * col_scale[None, :]).astype(jnp.bfloat16)


def raised(result, stream_key, source, target, blocks, factor):
    owner, partner = [(jnp.arange(result.shape[axis_at]) // (result.shape[axis_at] // blocks)).reshape([-1 if axis == axis_at else 1 for axis in range(result.ndim)]) for axis_at in (source, target)]
    chosen = jax.random.permutation(stream_key, blocks)[partner]
    strong = (owner == chosen) | (owner == (partner + blocks // 2) % blocks)
    return jnp.where(strong, factor * result, result)


def steps_of(rng, dims, shards, smallest, largest):
    def one(dim, blocks):
        draws = jax.random.uniform(jax.random.fold_in(jax.random.fold_in(rng, 6), dim), (blocks,), jnp.float32, smallest / len(shards), largest / len(shards))
        return jnp.repeat(jnp.exp(draws), dims[dim] // blocks).reshape((-1,) + (1,) * (len(dims) - dim - 1))

    level = one(*shards[0])
    for cut in shards[1:]:
        level = level * one(*cut)
    return level


def bell_draw(stream_key, dims, spread, reach, cuts=(), held_as=jnp.bfloat16):
    loudness = steps_of(stream_key, dims, cuts, -0.22, 0.18) if cuts else 1.0
    array = jax.random.normal(stream_key, dims, jnp.float32) * spread * loudness
    return jnp.minimum(jnp.maximum(array, -reach), reach).astype(held_as)


def bell_draw_with(own_key, extent, scale, reach, cuts, heavy, held_as=jnp.bfloat16):
    values = scale * jax.random.normal(own_key, extent, jnp.float32)
    if cuts:
        values = values * steps_of(own_key, extent, cuts, -0.22, 0.18)
    return jnp.clip(raised(values, jax.random.fold_in(own_key, 3), *heavy), -reach, reach).astype(held_as)


def setup_inputs(seed: int = 0) -> dict:
    arg_keys = jax.random.split(jax.random.key(seed), 4)
    return {
        "momentum": draw_momentum(jax.random.fold_in(arg_keys[3], 71), 0),
        "gradient": bell_draw_with(arg_keys[1], (M_ROWS, N_COLS), 1.0, 6.0, ((0, 16), (1, 8)), (0, 1, 16, 2.0)),
        "right_factor": bell_draw(arg_keys[2], (N_COLS, RANK), N_COLS ** -0.5, 0.0390625, ((0, 8),)),
    }


keep_rate = 0.95
epsilon = 1e-06

def reference(momentum, gradient, right_factor):
    buffer_sum = (momentum.astype(jnp.float32) + gradient.astype(jnp.float32)).astype(jnp.bfloat16)
    product = jnp.dot(buffer_sum.astype(jnp.float32), right_factor.astype(jnp.float32), preferred_element_type=jnp.float32)
    gram_total = jnp.dot(product.T, product, precision=lax.Precision.HIGHEST)
    lower_factor = jnp.linalg.cholesky(gram_total)
    orthonormal = jax.scipy.linalg.solve_triangular(lower_factor, product.T, lower=True).T.astype(jnp.bfloat16)
    right_full = lax.dot_general(buffer_sum.astype(jnp.float32), orthonormal.astype(jnp.float32), (((0,), (0,)), ((), ())), preferred_element_type=jnp.float32)
    right_round = right_full.astype(jnp.bfloat16)
    col_squares = lax.optimization_barrier(jnp.sum(right_full * right_full, axis=0))
    new_factor = (right_full * lax.rsqrt(col_squares + epsilon)).astype(jnp.bfloat16)
    feedback = lax.dot_general(orthonormal.astype(jnp.float32), right_round.astype(jnp.float32), (((1,), (1,)), ((), ())), preferred_element_type=jnp.float32)
    new_momentum = (buffer_sum.astype(jnp.float32) - (1.0 - keep_rate) * feedback).astype(jnp.bfloat16)
    rms_scale = math.sqrt(M_ROWS * N_COLS / RANK)
    low_rank = lax.dot_general(orthonormal.astype(jnp.float32), new_factor.astype(jnp.float32), (((1,), (1,)), ((), ())), preferred_element_type=jnp.float32)
    update = (low_rank * rms_scale).astype(jnp.bfloat16)
    return (new_momentum, new_factor, update)
```

```python
import functools
import math

import jax
import jax.numpy as jnp
from jax import lax
from jax.experimental import pallas as pl
from jax.experimental.pallas import tpu as pltpu
from jax.sharding import PartitionSpec as P

M_ROWS = 14336
N_COLS = 26624
RANK = 256

keep_rate = 0.95
epsilon = 1e-06

F32, BF = jnp.float32, jnp.bfloat16
COL_T = F32
PARTS = 2
ROW_T = F32
NN, NT, TN = ((1,), (0,)), ((1,), (1,)), ((0,), (0,))
DIAG = 64
MiB = 2**20


def dot(a, b, dims):
    return lax.dot_general(a, b, (dims, ((), ())), preferred_element_type=F32)


def split(a):
    hi = a.astype(BF)
    return hi, (a - hi.astype(F32)).astype(BF)


def dot3(a, b, dims):
    a_hi, a_lo = split(a)
    b_hi, b_lo = split(b)
    return dot(a_hi, b_hi, dims) + (dot(a_hi, b_lo, dims) + dot(a_lo, b_hi, dims))


def block_inverse(a):
    n, q = DIAG, 8
    eye = (
        lax.broadcasted_iota(jnp.int32, (n, n), 0) == lax.broadcasted_iota(jnp.int32, (n, n), 1)
    ).astype(F32)
    m = jnp.concatenate([a, eye], axis=1)
    groups = [m[q * g : q * g + q] for g in range(n // q)]
    sub = lax.broadcasted_iota(jnp.int32, (q, 2 * n), 0)
    full = (q, 2 * n)
    for g in range(n // q):
        j = g * q
        rows = [jnp.broadcast_to(groups[g][t : t + 1], full) for t in range(q)]
        cols = [
            [jnp.broadcast_to(group[:, j + t : j + t + 1], full) for t in range(q)]
            for group in groups[g:]
        ]
        small = [
            [jnp.broadcast_to(cols[0][t][s : s + 1], full) for t in range(s + 1)] for s in range(q)
        ]
        inv = []
        for t in range(q):
            inv.append(1.0 / small[t][t])
            for s in range(t + 1, q):
                f = small[s][t] * inv[t]
                for u in range(t + 1, s + 1):
                    small[s][u] = small[s][u] - f * small[u][t]
                rows[s] = rows[s] - f * rows[t]
                for col in cols[1:]:
                    col[s] = col[s] - f * col[t]
        scaled = [rows[t] * inv[t] for t in range(q)]
        for h in range(g + 1, n // q):
            for t in range(q):
                groups[h] = groups[h] - cols[h - g][t] * scaled[t]
        new = groups[g]
        for t in range(q):
            new = jnp.where(sub == t, rows[t] * lax.rsqrt(small[t][t]), new)
        groups[g] = new
    return jnp.concatenate([group[:, n:] for group in groups], axis=0)


def cholesky_step(k, g_ref, l_ref, x_ref):
    lo, hi = k * DIAG, (k + 1) * DIAG
    inv = block_inverse(g_ref[lo:hi, lo:hi])
    x_ref[lo:hi, lo:hi] = inv
    if hi < RANK:
        below = dot3(g_ref[hi:, lo:hi], inv, NT)
        l_ref[hi:, lo:hi] = below
        g_ref[hi:, hi:] -= dot3(below, below, NT)
    if k:
        left = dot3(l_ref[lo:hi, :lo], x_ref[:lo, :lo], NN)
        x_ref[lo:hi, :lo] = -dot3(inv, left, NN)


def factor_kernel(
    m_in, g_in, v_in, b_out, q_out, r_out, s_out,
    mb, gb, vb, part, crecv, zsend, zrecv, pg, gy, gx, gf, gs, ls, xs, w, w1, w2, r, sq, qb, sb,
    load_sem, store_sem, send_sem, recv_sem,
):
    row, col = lax.axis_index("row"), lax.axis_index("col")
    x, y, z, c = row // 4, row % 4, col // 2, col % 2
    n_blk = r.shape[3]
    n_a = (n_blk // 2 + 15) // 16 * 16
    quarter = mb.shape[1]
    rows_own = quarter // 2

    def at_z(d):
        return (row, 2 * ((z + d) % 4) + c)

    def at_x(d):
        return (4 * ((x + d) % 4) + y, col)

    def at_y(d):
        return (4 * x + (y + d) % 4, col)

    sibling = (row, 2 * z + 1 - c)
    at = {"x": at_x, "y": at_y, "z": at_z}
    me = {"x": x, "y": y, "z": z}

    started = []

    def send(src, dst, device):
        k = len(started)
        copy = pltpu.make_async_remote_copy(
            src_ref=src, dst_ref=dst, send_sem=send_sem.at[k], recv_sem=recv_sem.at[k],
            device_id=device, device_id_type=pl.DeviceIdType.MESH,
        )
        copy.start()
        started.append(copy)
        return copy

    v_load = pltpu.make_async_copy(v_in, vb, load_sem.at[8])
    v_load.start()
    loads = []
    for s in range(4):
        zt = (z + s + 1) % 4
        at_rows = pl.ds(pl.multiple_of(zt * quarter, quarter), quarter)
        pair = (
            pltpu.make_async_copy(m_in.at[at_rows, :], mb.at[zt], load_sem.at[2 * s]),
            pltpu.make_async_copy(g_in.at[at_rows, :], gb.at[zt], load_sem.at[2 * s + 1]),
        )
        for copy in pair:
            copy.start()
        loads.append(pair)

    barrier = pltpu.get_barrier_semaphore()
    partners = [sibling] + [at[a](d) for a in "xyz" for d in (1, 2, 3)]
    for device in partners:
        pl.semaphore_signal(barrier, inc=1, device_id=device, device_id_type=pl.DeviceIdType.MESH)
    pl.semaphore_wait(barrier, len(partners))

    to_sibling, to_z = [], []

    def pass_on(s):
        zt = (z + s + 1) % 4
        to_sibling[s].wait_recv()
        total = part[zt, c] + crecv[s]
        if s < 3:
            zsend[s] = total.astype(COL_T)
            to_z.append(send(zsend.at[s], zrecv.at[s], at_z(s + 1)))
        return total

    v_load.wait()
    for s in range(4):
        zt = (z + s + 1) % 4
        for copy in loads[s]:
            copy.wait()
        total = (mb[zt].astype(F32) + gb[zt].astype(F32)).astype(BF)
        mb[zt] = total
        part[zt] = dot(total, vb[...], NN).reshape(2, rows_own, RANK)
        to_sibling.append(send(part.at[zt, 1 - c], crecv.at[s], sibling))
        if s:
            pass_on(s - 1)
    stores = []

    def store(src, dst):
        copy = pltpu.make_async_copy(src, dst, store_sem.at[len(stores)])
        copy.start()
        stores.append(copy)

    for s in range(4):
        store(mb.at[s], b_out.at[s])
    own = pass_on(3)
    for s in range(3):
        to_z[s].wait_recv()
        own = own + zrecv[s].astype(F32)

    pg[0, z, c] = own.astype(BF)
    if PARTS == 2:
        pg[1, z, c] = split(own)[1]
    mine = pg.at[:, z, c]
    from_z = [send(mine, mine, at_z(d)) for d in (2, 1, 3)]
    from_sibling = [send(mine, mine, sibling)]
    for d, copy in zip((2, 1, 3), from_z):
        copy.wait_recv()
        there = pg.at[:, (z - d) % 4, c]
        from_sibling.append(send(there, there, sibling))
    for copy in from_sibling:
        copy.wait_recv()

    p_hi = pg[0].reshape(4 * quarter, RANK)
    gram = dot(p_hi, p_hi, TN)
    if PARTS == 2:
        p_lo = pg[1].reshape(4 * quarter, RANK)
        cross = dot(p_hi, p_lo, TN)
        gram = gram + (cross + cross.T)
    gs[...] = gram

    def spread(buf, axis):
        here = buf.at[me[axis]]
        return [send(here, here, at[axis](d)) for d in (2, 1, 3)]

    def collect(buf, copies):
        for copy in copies:
            copy.wait_recv()
        return (buf[0] + buf[1]) + (buf[2] + buf[3])

    gy[y] = gs[pl.ds(pl.multiple_of(col * 32, 32), 32), :]
    gram_y = spread(gy, "y")

    half = 8 * n_blk

    def right_part(i):
        b = mb[:, :, i * half : (i + 1) * half].reshape(4 * quarter, half)
        out = dot(b, p_hi, TN)
        if PARTS == 2:
            out = out + dot(b, p_lo, TN)
        for h in range(2):
            w[h, 2 * i : 2 * i + 2] = (
                out[:, 128 * h : 128 * h + 128].reshape(2, 4, n_blk, 128).astype(ROW_T)
            )

    right_part(0)
    gx[x] = collect(gy, gram_y)
    gram_x = spread(gx, "x")
    right_part(1)

    def ring(stage, h):
        axis = "xy"[(stage + h) % 2]
        i = me[axis]

        def chunk(d, part_b):
            j = (i + d) % 4
            if stage == 0:
                cut = slice(2, 4) if part_b else slice(0, 2)
                return w.at[0, j, cut] if h == 0 else w.at[1, cut, j]
            cut = pl.ds(n_a, n_blk - n_a) if part_b else pl.ds(0, n_a)
            return w.at[0, x, j, cut] if h == 0 else w.at[1, j, y, cut]

        def slot(k, part_b):
            if stage == 0:
                return w1.at[h, k]
            return w2.at[h, k, pl.ds(0, n_blk - n_a if part_b else n_a)]

        return at[axis], chunk, slot

    def ring_start(stage):
        flights = []
        for h in range(2):
            dev, chunk, slot = ring(stage, h)
            flights.append([
                send(chunk(2, False), slot(0, False), dev(1)),
                send(chunk(2, True), slot(1, True), dev(3)),
            ])
        for h in range(2):
            dev, chunk, slot = ring(stage, h)
            flights[h].append(send(chunk(1, True), slot(2, True), dev(1)))
            flights[h].append(send(chunk(3, False), slot(3, False), dev(3)))
        return flights

    def ring_merge(stage, flights):
        for h in range(2):
            dev, chunk, slot = ring(stage, h)
            for k, d, part_b in ((0, 1, False), (1, 3, True)):
                flights[h][k].wait_recv()
                here = slot(k, part_b)
                here[...] = (here[...].astype(F32) + chunk(d, part_b)[...].astype(F32)).astype(ROW_T)
                flights[h].append(send(here, slot(4 + k, part_b), dev(d)))

    def ring_finish(stage, flights):
        for h in range(2):
            dev, chunk, slot = ring(stage, h)
            for copy in flights[h][2:]:
                copy.wait_recv()
            for part_b, first, second in ((False, 3, 4), (True, 2, 5)):
                here = chunk(0, part_b)
                here[...] = (
                    here[...].astype(F32)
                    + (slot(first, part_b)[...].astype(F32) + slot(second, part_b)[...].astype(F32))
                ).astype(ROW_T)

    gf[col] = collect(gx, gram_x)
    here = gf.at[col]
    gram_z = [send(here, here, at_z(d)) for d in (2, 1, 3)]
    gram_c = [send(here, here, sibling)]
    flights = ring_start(0)
    for d, copy in zip((2, 1, 3), gram_z):
        copy.wait_recv()
        there = gf.at[2 * ((z - d) % 4) + c]
        gram_c.append(send(there, there, sibling))
    for copy in gram_c:
        copy.wait_recv()
    gs[...] = gf[...].reshape(RANK, RANK)
    xs[...] = jnp.zeros_like(xs)

    cholesky_step(0, gs, ls, xs)
    cholesky_step(1, gs, ls, xs)
    ring_merge(0, flights)
    cholesky_step(2, gs, ls, xs)
    cholesky_step(3, gs, ls, xs)
    ring_finish(0, flights)
    flights = ring_start(1)
    ring_merge(1, flights)
    x_hi, x_lo = split(xs[...])
    ring_finish(1, flights)

    summed = jnp.concatenate([w[0, x, y], w[1, x, y]], axis=1).astype(F32)
    s_hi, s_lo = split(summed)
    right = dot(s_hi, x_hi, NT) + (dot(s_hi, x_lo, NT) + dot(s_lo, x_hi, NT))
    r[0, x, y] = right[:, :128].astype(BF)
    r[1, x, y] = right[:, 128:].astype(BF)

    def block(h, d_first, d_second):
        if h == 0:
            return r.at[0, (x + d_second) % 4, (y + d_first) % 4]
        return r.at[1, (x + d_first) % 4, (y + d_second) % 4]

    first_dev, second_dev = (at_y, at_x), (at_x, at_y)
    to_first = [[], []]
    to_second = [[[], []], [[], []]]

    def second_send(h, d):
        here = block(h, d, 0)
        for direction, step in ((0, 1), (1, 3)):
            to_second[h][direction].append((d, send(here, here, second_dev[h](step))))

    for h in range(2):
        here = block(h, 0, 0)
        to_first[h] = [send(here, here, first_dev[h](d)) for d in (1, 3)]
    for h in range(2):
        second_send(h, 0)
    sq[0, y] = jnp.broadcast_to(jnp.sum(right * right, axis=0, keepdims=True), (8, RANK))
    squares = spread(sq.at[0], "y")

    if PARTS == 2:
        orthonormal = dot(p_hi, x_hi, NT) + (dot(p_hi, x_lo, NT) + dot(p_lo, x_hi, NT))
    else:
        orthonormal = dot(p_hi, x_hi, NT) + dot(p_hi, x_lo, NT)
    qb[...] = orthonormal.astype(BF)
    store(qb, q_out)

    relayed = [[], []]
    for h in range(2):
        for k, d, cut in ((0, 3, pl.ds(0, n_a)), (1, 1, pl.ds(n_a, n_blk - n_a))):
            to_first[h][k].wait_recv()
            there = block(h, d, 0).at[cut]
            relayed[h].append(send(there, there, first_dev[h](4 - d)))
            second_send(h, d)
    sq[1, x] = collect(sq.at[0], squares)
    squares = spread(sq.at[1], "x")
    for h in range(2):
        for copy in relayed[h]:
            copy.wait_recv()
        second_send(h, 2)
    sq[2, z] = collect(sq.at[1], squares)
    squares = spread(sq.at[2], "z")
    last = []
    for h in range(2):
        for i in range(4):
            for direction, d_second in ((0, 3), (1, 1)):
                d, copy = to_second[h][direction][i]
                copy.wait_recv()
                if (d in (0, 1)) == (direction == 0):
                    there = block(h, d, d_second)
                    last.append(send(there, there, second_dev[h](4 - d_second)))
    sq[3, c] = collect(sq.at[2], squares)
    here = sq.at[3, c]
    squares = send(here, here, sibling)
    for copy in last:
        copy.wait_recv()
    store(r, r_out)
    squares.wait_recv()
    sb[...] = lax.rsqrt(sq[3, 0] + sq[3, 1] + epsilon)
    store(sb, s_out)
    for copy in started:
        copy.wait_send()
    for copy in stores:
        copy.wait()


def output_kernel(b_ref, q_ref, r_ref, s_ref, momentum_ref, factor_ref, update_ref):
    q = q_ref[...]
    right_round = jnp.concatenate([r_ref[0], r_ref[1]], axis=1)
    new_factor = (right_round.astype(F32) * s_ref[0:1]).astype(BF)
    factor_ref[...] = new_factor
    feedback = dot(q, right_round, NT)
    momentum_ref[...] = (b_ref[...].astype(F32) - (1.0 - keep_rate) * feedback).astype(BF)
    rms_scale = math.sqrt(M_ROWS * N_COLS / RANK)
    update_ref[...] = (dot(q, new_factor, NT) * rms_scale).astype(BF)


def per_device(momentum, gradient, right_factor):
    rows, cols = momentum.shape
    quarter, n_blk = rows // 4, cols // 16
    n_a = (n_blk // 2 + 15) // 16 * 16
    hbm = pl.BlockSpec(memory_space=pl.ANY)
    vm = pltpu.VMEM
    sends = 4 + 3 + 7 + 6 + 7 + 24 + 4 + 4 + 16 + 8 + 10
    buffer_sum, orthonormal, right_round, scale = pl.pallas_call(
        factor_kernel,
        name="factors",
        out_shape=(
            jax.ShapeDtypeStruct((4, quarter, cols), BF),
            jax.ShapeDtypeStruct((rows, RANK), BF),
            jax.ShapeDtypeStruct((2, 4, 4, n_blk, 128), BF),
            jax.ShapeDtypeStruct((8, RANK), F32),
        ),
        in_specs=[hbm] * 3,
        out_specs=(hbm,) * 4,
        scratch_shapes=[
            vm((4, quarter, cols), BF),
            vm((4, quarter, cols), BF),
            vm((cols, RANK), BF),
            vm((4, 2, quarter // 2, RANK), F32),
            vm((4, quarter // 2, RANK), F32),
            vm((3, quarter // 2, RANK), COL_T),
            vm((3, quarter // 2, RANK), COL_T),
            vm((PARTS, 4, 2, quarter // 2, RANK), BF),
            vm((4, 32, RANK), F32),
            vm((4, 32, RANK), F32),
            vm((8, 32, RANK), F32),
            vm((RANK, RANK), F32),
            vm((RANK, RANK), F32),
            vm((RANK, RANK), F32),
            vm((2, 4, 4, n_blk, 128), ROW_T),
            vm((2, 6, 2, n_blk, 128), ROW_T),
            vm((2, 6, n_a, 128), ROW_T),
            vm((2, 4, 4, n_blk, 128), BF),
            vm((4, 4, 8, RANK), F32),
            vm((rows, RANK), BF),
            vm((8, RANK), F32),
            pltpu.SemaphoreType.DMA((9,)),
            pltpu.SemaphoreType.DMA((8,)),
            pltpu.SemaphoreType.DMA((sends,)),
            pltpu.SemaphoreType.DMA((sends,)),
        ],
        compiler_params=pltpu.CompilerParams(
            collective_id=0, has_side_effects=True, vmem_limit_bytes=56 * MiB
        ),
    )(momentum, gradient, right_factor)
    tile = 256
    whole = functools.partial(pl.BlockSpec, index_map=lambda i: (0, 0))
    columns = pl.BlockSpec((rows, tile), lambda i: (0, i))
    new_momentum, new_factor, update = pl.pallas_call(
        output_kernel,
        name="outputs",
        grid=(cols // tile,),
        out_shape=(
            jax.ShapeDtypeStruct((rows, cols), BF),
            jax.ShapeDtypeStruct((cols, RANK), BF),
            jax.ShapeDtypeStruct((rows, cols), BF),
        ),
        in_specs=[
            columns,
            whole((rows, RANK)),
            pl.BlockSpec((2, tile, 128), lambda i: (0, i, 0)),
            whole((8, RANK)),
        ],
        out_specs=(columns, pl.BlockSpec((tile, RANK), lambda i: (i, 0)), columns),
        compiler_params=pltpu.CompilerParams(vmem_limit_bytes=32 * MiB),
    )(buffer_sum.reshape(rows, cols), orthonormal, right_round.reshape(2, cols, 128), scale)
    return (new_momentum, new_factor, update)


def solution(mesh):
    placed = (P("row", "col"), P("row", "col"), P("col", None))
    return jax.shard_map(
        per_device,
        mesh=mesh,
        in_specs=placed,
        out_specs=(P("row", "col"), P("col", None), P("row", "col")),
        check_vma=False,
    )
```
